32 devices in a mesh: pairs: 2 (over x), tgt: 16 (over z, y, core).
Axes of the slice: x: 2, y: 2, z: 4, core: 2. Of those that a mesh axis runs over, the one named last changes fastest.
Arguments:
- src_hidden: bfloat16 [4096, 128], P(('pairs', 'tgt')), parts along dimension 0, may hold values from -6 to 6
- tgt_hidden: bfloat16 [256, 256, 128], P(('pairs', 'tgt')), parts along dimension 0, may hold values from -6 to 6
- proj_weight: bfloat16 [128, 256], replicated, may hold values from -0.5 to 0.5
- proj_bias: float32 [256], replicated, may hold values from -1.5 to 1.5
Outputs:
- level_one: bfloat16 [128, 128, 2048], P(('pairs', 'tgt')), parts along dimension 0
- level_two: bfloat16 [4096, 2048], P(('pairs', 'tgt')), parts along dimension 0
- level_three: bfloat16 [4096, 512], P(('pairs', 'tgt')), parts along dimension 0
The draws below stay inside these ranges and needn't reach their ends.
There are 2 independent parts, one for each index of `pairs`. The reference program is written for one: setup_inputs(seed, part) draws one part's arguments, and reference() takes and returns one part's arrays. A program takes and returns all parts, laid end to end along the dimension named above; an argument that names none is the same for every part. Nothing has to cross between parts.
All inputs are finite; a program needn't handle non-finite values.
Results may differ from the reference program's by a relative error of at most 0.006.
Values may be sent and summed in bfloat16 or wider, within the bound.
A program may use at most 64 MiB of HBM per device.

```python
import math
import jax
import jax.numpy as jnp
from jax import lax

CH = 256
HID = 128
IMG_W = 256
IMG_H = 128
SRC = 2048


def block_scale(own_key, dims, split, low, largest):
    loudness = 1.0
    for dim, blocks in split:
        draws = jax.random.uniform(jax.random.fold_in(jax.random.fold_in(own_key, 6), dim), (blocks,), jnp.float32, low / len(split), largest / len(split))
        loudness = loudness * jnp.repeat(jnp.exp(draws), dims[dim] // blocks).reshape((-1,) + (1,) * (len(dims) - 1 - dim))
    return loudness


def bell_draw(key, shape, deviation, limit, pieces=(), held_as=jnp.bfloat16):
    drawn = jax.random.normal(key, shape, jnp.float32) * deviation
    if len(pieces) > 0:
        drawn = block_scale(key, shape, pieces, -0.22, 0.18) * drawn
    return jnp.clip(drawn, min=-limit, max=limit).astype(held_as)


def setup_inputs(seed: int = 0, part: int = 0) -> dict:
    key_of = jax.random.split(jax.random.key(seed), 5)
    part_keys = jax.random.split(jax.random.fold_in(key_of[4], part), 5)
    src_hidden = bell_draw(part_keys[0], (SRC, HID), 1.0, 6.0, ((0, 16),))
    tgt_hidden = bell_draw(part_keys[1], (IMG_H, IMG_W, HID), 1.0, 6.0, ((0, 16),))
    proj_weight = bell_draw(key_of[2], (HID, CH), HID ** -0.5, 0.5)
    proj_bias = bell_draw(key_of[3], (CH,), 0.25, 1.5, (), jnp.float32)
    return {"src_hidden": src_hidden, "tgt_hidden": tgt_hidden, "proj_weight": proj_weight, "proj_bias": proj_bias}


def project_features(hidden, weight, bias):
    flat = hidden.reshape(-1, hidden.shape[-1])
    result = jnp.dot(flat, weight, preferred_element_type=jnp.float32) + bias
    return result.astype(jnp.bfloat16).reshape(hidden.shape[:-1] + (weight.shape[1],))

def average_pool(values):
    height, across, depth = values.shape
    return values.reshape(height // 2, 2, across // 2, 2, depth).mean(axis=(1, 3))

def reference(src_hidden, tgt_hidden, proj_weight, proj_bias):
    src_feat = project_features(src_hidden, proj_weight, proj_bias)
    tgt_feat = project_features(tgt_hidden, proj_weight, proj_bias)
    inverse_root = 1.0 / math.sqrt(CH)
    row_blocks = tgt_feat.reshape(IMG_H // 8, 8 * IMG_W, CH)

    def one_block(block_feat):
        correlation = jnp.dot(block_feat, src_feat.T, preferred_element_type=jnp.float32) * inverse_root
        correlation = correlation.reshape(8, IMG_W, SRC)
        pooled_once = average_pool(correlation)
        pooled_twice = average_pool(pooled_once)
        return (pooled_once.astype(jnp.bfloat16), pooled_twice.astype(jnp.bfloat16))
    one_blocks, two_blocks = lax.map(one_block, row_blocks)
    level_one = one_blocks.reshape(IMG_H // 2, IMG_W // 2, SRC)
    coarse_grid = two_blocks.reshape(IMG_H // 4, IMG_W // 4, SRC)
    level_two = jnp.transpose(coarse_grid, (2, 0, 1)).reshape(SRC, IMG_H // 4 * (IMG_W // 4))
    pooled_thrice = average_pool(coarse_grid.astype(jnp.float32))
    level_three = jnp.transpose(pooled_thrice, (2, 0, 1)).reshape(SRC, IMG_H // 8 * (IMG_W // 8)).astype(jnp.bfloat16)
    return (level_one, level_two, level_three)
```

```python
import functools
import math

import jax
import jax.numpy as jnp
from jax import lax
from jax.experimental import pallas as pl
from jax.experimental.pallas import tpu as pltpu
from jax.sharding import PartitionSpec as P

MESH = pl.DeviceIdType.MESH
LAST = (((1,), (1,)), ((), ()))


def dot(left, right):
    return jnp.dot(left, right, preferred_element_type=jnp.float32)


def dot_last(left, right):
    return lax.dot_general(left, right, LAST, preferred_element_type=jnp.float32)


def split_parts(values):
    upper = values.astype(jnp.bfloat16)
    lower = (values - upper.astype(jnp.float32)).astype(jnp.bfloat16)
    return upper, lower


def pool_matrix(window, width):
    shape = (width // window, window * width)
    out = lax.broadcasted_iota(jnp.int32, shape, 0)
    pixel = lax.broadcasted_iota(jnp.int32, shape, 1)
    inside = lax.div(lax.rem(pixel, width), window) == out
    return jnp.where(inside, 1.0 / (window * window), 0.0).astype(jnp.bfloat16)


def gather_kernel(count, scale, src_ref, tgt_ref, weight_ref, bias_ref,
                  all_ref, fine_ref, send_sem, recv_sem):
    rows, width, hidden = tgt_ref.shape
    lines = count // 4
    me = lax.axis_index("tgt")
    core = lax.rem(me, 2)
    mate = me + 1 - 2 * core
    side = lax.rem(lax.div(me, 2), 2)
    beside = me + 2 - 4 * side
    line = lax.div(me, 4)
    place = me - 4 * line

    def along(step):
        return 4 * lax.rem(line + step, lines) + place

    barrier = pltpu.get_barrier_semaphore()
    peers = [along(step) for step in range(1, lines)] + [beside, mate]
    for peer in peers:
        pl.semaphore_signal(barrier, inc=1, device_id={"tgt": peer}, device_id_type=MESH)
    all_ref[me, 0] = src_ref[...]
    pl.semaphore_wait(barrier, len(peers))

    sent = []

    def copy(part, block, peer, slot):
        return pltpu.make_async_remote_copy(
            src_ref=all_ref.at[block, part],
            dst_ref=all_ref.at[block, part],
            send_sem=send_sem.at[part, slot],
            recv_sem=recv_sem.at[part, block],
            device_id={"tgt": peer},
            device_id_type=MESH,
        )

    slots = [0, 0]

    def send(part, block, peer):
        one = copy(part, block, peer, slots[part])
        slots[part] += 1
        one.start()
        sent.append(one)

    def arrive(part, block):
        copy(part, block, mate, 0).wait_recv()

    def own(part):
        for step in range(1, lines):
            send(part, me, along(step))
        send(part, me, beside)
        send(part, me, mate)

    own(0)
    coarse = pool_matrix(4, width)
    pooled = []
    for row in range(0, rows, 4):
        pooled.append(dot(coarse, tgt_ref[row:row + 4].reshape(4 * width, hidden)))
    all_ref[me, 1] = jnp.concatenate(pooled, axis=0).astype(jnp.bfloat16)
    own(1)
    fine = pool_matrix(2, width)
    half = width // 2
    for row in range(0, rows, 2):
        upper, lower = split_parts(dot(fine, tgt_ref[row:row + 2].reshape(2 * width, hidden)))
        feat = dot(upper, weight_ref[...]) + dot(lower, weight_ref[...]) + bias_ref[...]
        fine_ref[row // 2 * half:(row // 2 + 1) * half] = (feat * scale).astype(jnp.bfloat16)
    for part in (0, 1):
        for step in range(1, lines):
            block = along(lines - step)
            arrive(part, block)
            send(part, block, beside)
            send(part, block, mate)
    for part in (0, 1):
        for step in range(lines):
            block = along((lines - step) % lines) + 2 - 4 * side
            arrive(part, block)
            send(part, block, mate)
    for part in (0, 1):
        for step in range(lines):
            block = along((lines - step) % lines) + 1 - 2 * core
            arrive(part, block)
            arrive(part, block + 2 - 4 * side)
    for one in sent:
        one.wait_send()


def level_kernel(scale, all_ref, fine_ref, src_ref, weight_ref, bias_ref,
                 one_ref, two_ref, three_ref, upper_ref, lower_ref, bias_dot_ref):
    group, _, block, hidden = all_ref.shape

    @pl.when(pl.program_id(0) == 0)
    def _():
        feat = (dot(src_ref[...], weight_ref[...]) + bias_ref[...]).astype(jnp.bfloat16)
        back = dot_last(feat, weight_ref[...]) * scale
        upper, lower = split_parts(back)
        upper_ref[...] = upper
        lower_ref[...] = lower
        shift = jnp.sum(feat.astype(jnp.float32) * bias_ref[...], axis=1, keepdims=True) * scale
        bias_dot_ref[...] = jnp.broadcast_to(shift, bias_dot_ref.shape)

    coarse = all_ref[:, 1].reshape(group * block, hidden)
    two = dot_last(upper_ref[...], coarse) + dot_last(lower_ref[...], coarse)
    two = (two + bias_dot_ref[:, :1]).astype(jnp.bfloat16)
    two_ref[...] = two
    wide = two_ref.shape[1]
    narrow = three_ref.shape[1]
    across = block // 2
    pixel = lax.broadcasted_iota(jnp.int32, (wide, narrow), 0)
    out = lax.broadcasted_iota(jnp.int32, (wide, narrow), 1)
    inside = (lax.div(pixel, block) * (across // 2) + lax.div(lax.rem(pixel, across), 2)) == out
    pool = jnp.where(inside, 0.25, 0.0).astype(jnp.bfloat16)
    three_ref[...] = dot(two, pool).astype(jnp.bfloat16)
    src = all_ref[:, 0].reshape(group * block, hidden)
    feat = (dot(src, weight_ref[...]) + bias_ref[...]).astype(jnp.bfloat16)
    one_ref[...] = dot_last(fine_ref[...], feat).astype(jnp.bfloat16)


def per_device(src_hidden, tgt_hidden, proj_weight, proj_bias):
    rows, width, hidden = tgt_hidden.shape
    channels = proj_weight.shape[1]
    count = lax.axis_size("tgt")
    own = src_hidden.shape[0]
    scale = 1.0 / math.sqrt(channels)
    fine_count = rows * width // 4
    bias = proj_bias.reshape(1, channels)
    vmem = pl.BlockSpec(memory_space=pltpu.VMEM)
    gathered, fine = pl.pallas_call(
        functools.partial(gather_kernel, count, scale),
        out_shape=(
            jax.ShapeDtypeStruct((count, 2, own, hidden), jnp.bfloat16),
            jax.ShapeDtypeStruct((fine_count, channels), jnp.bfloat16),
        ),
        in_specs=[vmem] * 4,
        out_specs=(vmem, vmem),
        scratch_shapes=[
            pltpu.SemaphoreType.DMA((2, count)),
            pltpu.SemaphoreType.DMA((2, count)),
        ],
        compiler_params=pltpu.CompilerParams(
            collective_id=0, has_side_effects=True, vmem_limit_bytes=32 * 1024 * 1024
        ),
        name="gather",
    )(src_hidden, tgt_hidden, proj_weight, bias)
    group = 4
    whole = lambda step: (0, 0)
    one, two, three = pl.pallas_call(
        functools.partial(level_kernel, scale),
        grid=(count // group,),
        out_shape=(
            jax.ShapeDtypeStruct((fine_count, own * count), jnp.bfloat16),
            jax.ShapeDtypeStruct((own, fine_count // 4 * count), jnp.bfloat16),
            jax.ShapeDtypeStruct((own, fine_count // 16 * count), jnp.bfloat16),
        ),
        in_specs=[
            pl.BlockSpec((group, 2, own, hidden), lambda step: (step, 0, 0, 0)),
            pl.BlockSpec((fine_count, channels), whole),
            pl.BlockSpec((own, hidden), whole),
            pl.BlockSpec((hidden, channels), whole),
            pl.BlockSpec((1, channels), whole),
        ],
        out_specs=(
            pl.BlockSpec((fine_count, own * group), lambda step: (0, step)),
            pl.BlockSpec((own, fine_count // 4 * group), lambda step: (0, step)),
            pl.BlockSpec((own, fine_count // 16 * group), lambda step: (0, step)),
        ),
        scratch_shapes=[
            pltpu.VMEM((own, hidden), jnp.bfloat16),
            pltpu.VMEM((own, hidden), jnp.bfloat16),
            pltpu.VMEM((own, 128), jnp.float32),
        ],
        compiler_params=pltpu.CompilerParams(vmem_limit_bytes=32 * 1024 * 1024),
        name="levels",
    )(gathered, fine, src_hidden, proj_weight, bias)
    return one.reshape(rows // 2, width // 2, own * count), two, three


def solution(mesh):
    return jax.shard_map(
        per_device,
        mesh=mesh,
        in_specs=(P(("pairs", "tgt"), None), P(("pairs", "tgt"), None, None), P(), P()),
        out_specs=(
            P(("pairs", "tgt"), None, None),
            P(("pairs", "tgt"), None),
            P(("pairs", "tgt"), None),
        ),
        check_vma=False,
    )
```

```python
import functools
import math

import jax
import jax.numpy as jnp
from jax import lax
from jax.experimental import pallas as pl
from jax.experimental.pallas import tpu as pltpu
from jax.sharding import PartitionSpec as P

MESH = pl.DeviceIdType.MESH
LAST = (((1,), (1,)), ((), ()))


def dot(left, right):
    return jnp.dot(left, right, preferred_element_type=jnp.float32)


def dot_last(left, right):
    return lax.dot_general(left, right, LAST, preferred_element_type=jnp.float32)


def split_parts(values):
    upper = values.astype(jnp.bfloat16)
    lower = (values - upper.astype(jnp.float32)).astype(jnp.bfloat16)
    return upper, lower


def pool_matrix(window, width):
    shape = (width // window, window * width)
    out = lax.broadcasted_iota(jnp.int32, shape, 0)
    pixel = lax.broadcasted_iota(jnp.int32, shape, 1)
    inside = lax.div(lax.rem(pixel, width), window) == out
    return jnp.where(inside, 1.0 / (window * window), 0.0).astype(jnp.bfloat16)


def gather_kernel(count, scale, src_hbm, tgt_hbm, weight_hbm, bias_hbm,
                  all_ref, one_ref, upper_ref, lower_ref, shift_ref,
                  tgt_ref, weight_ref, bias_ref, fine_ref, load_sem, send_sem, recv_sem):
    rows, width, hidden = tgt_ref.shape
    own = src_hbm.shape[0]
    lines = count // 4
    me = lax.axis_index("tgt")
    core = lax.rem(me, 2)
    to_mate = 1 - 2 * core
    side = lax.rem(lax.div(me, 2), 2)
    to_beside = 2 - 4 * side
    line = lax.div(me, 4)
    has_above = line + 1 < lines
    has_below = line > 0

    barrier = pltpu.get_barrier_semaphore()

    def greet(peer):
        pl.semaphore_signal(barrier, inc=1, device_id={"tgt": peer}, device_id_type=MESH)

    greet(me + to_mate)
    greet(me + to_beside)
    pl.when(has_above)(lambda: greet(me + 4))
    pl.when(has_below)(lambda: greet(me - 4))
    loads = [
        pltpu.make_async_copy(tgt_hbm, tgt_ref, load_sem.at[0]),
        pltpu.make_async_copy(weight_hbm, weight_ref, load_sem.at[1]),
        pltpu.make_async_copy(bias_hbm, bias_ref, load_sem.at[2]),
        pltpu.make_async_copy(src_hbm, all_ref.at[me, 0], load_sem.at[3]),
    ]
    for load in loads:
        load.start()
    links = 2 + jnp.where(has_above, 1, 0) + jnp.where(has_below, 1, 0)
    pl.semaphore_wait(barrier, links)

    sent = []
    slots = [0, 0]

    def copy(part, block, peer, slot, first=False):
        return pltpu.make_async_remote_copy(
            src_ref=src_hbm if first else all_ref.at[block, part],
            dst_ref=all_ref.at[block, part],
            send_sem=send_sem.at[part, slot],
            recv_sem=recv_sem.at[part, block],
            device_id={"tgt": peer},
            device_id_type=MESH,
        )

    def send(part, block, peer, when, first=False):
        slot = slots[part]
        slots[part] += 1
        go = lambda: copy(part, block, peer, slot, first).start()
        end = lambda: copy(part, block, peer, slot, first).wait_send()
        sent.append((when, end))
        return go

    def arrive(part, block):
        copy(part, block, me + to_mate, 0).wait_recv()

    def level_one(block):
        feat = (dot(all_ref[block, 0], weight_ref[...]) + bias_ref[...]).astype(jnp.bfloat16)
        at = pl.ds(pl.multiple_of(block * own, own), own)
        one_ref[:, at] = dot_last(fine_ref[...], feat).astype(jnp.bfloat16)
        return feat

    def own_block(part):
        first = part == 0
        pl.when(has_above)(send(part, me, me + 4, has_above, first))
        pl.when(has_below)(send(part, me, me - 4, has_below, first))
        send(part, me, me + to_beside, None, first)()
        send(part, me, me + to_mate, None, first)()

    own_block(0)
    coarse = pool_matrix(4, width)
    loads[0].wait()
    pooled = []
    for row in range(0, rows, 4):
        pooled.append(dot(coarse, tgt_ref[row:row + 4].reshape(4 * width, hidden)))
    all_ref[me, 1] = jnp.concatenate(pooled, axis=0).astype(jnp.bfloat16)
    own_block(1)
    fine = pool_matrix(2, width)
    half = width // 2
    for load in loads[1:]:
        load.wait()
    for row in range(0, rows, 2):
        upper, lower = split_parts(dot(fine, tgt_ref[row:row + 2].reshape(2 * width, hidden)))
        feat = dot(upper, weight_ref[...]) + dot(lower, weight_ref[...]) + bias_ref[...]
        fine_ref[row // 2 * half:(row // 2 + 1) * half] = (feat * scale).astype(jnp.bfloat16)
    feat = level_one(me)
    upper, lower = split_parts(dot_last(feat, weight_ref[...]) * scale)
    upper_ref[...] = upper
    lower_ref[...] = lower
    shift = jnp.sum(feat.astype(jnp.float32) * bias_ref[...], axis=1, keepdims=True) * scale
    shift_ref[...] = jnp.broadcast_to(shift, shift_ref.shape)

    def from_line(part, step, sign):
        block = me + 4 * step * sign
        there = (line >= step) if sign < 0 else (line + step < lines)
        onward = has_above if sign < 0 else has_below
        both = jnp.logical_and(there, onward)
        relay = send(part, block, me - 4 * sign, both)
        across = send(part, block, me + to_beside, there)
        inner = send(part, block, me + to_mate, there)

        @pl.when(there)
        def _():
            arrive(part, block)
            pl.when(onward)(relay)
            across()
            inner()

        if part == 0:
            return lambda: pl.when(there)(lambda: (level_one(block), None)[1])
        return lambda: None

    def from_beside(part, step, sign):
        block = me + to_beside + 4 * step * sign
        there = (line >= step) if sign < 0 else (line + step < lines)
        inner = send(part, block, me + to_mate, there)

        @pl.when(there)
        def _():
            arrive(part, block)
            inner()
            if part == 0:
                level_one(block)

    def beside_step(step):
        for part in (0, 1):
            from_beside(part, step, -1)
            if step:
                from_beside(part, step, 1)

    for step in range(1, lines):
        later = []
        for part in (0, 1):
            for sign in (-1, 1):
                later.append(from_line(part, step, sign))
        for work in later:
            work()
        beside_step(step - 1)
    beside_step(lines - 1)
    other = me + to_mate - 4 * line
    for part in (0, 1):
        for step in range(lines):
            for block in (other + 4 * step, other + 4 * step + to_beside):
                arrive(part, block)
                if part == 0:
                    level_one(block)
    for when, end in sent:
        if when is None:
            end()
        else:
            pl.when(when)(end)


def level_kernel(group, all_ref, one_ref, upper_ref, lower_ref, shift_ref,
                 one_hbm, two_hbm, three_hbm, two_ref, three_ref, sems):
    count, _, block, hidden = all_ref.shape
    rows = one_ref.shape[0] // 4
    copies = []

    def put(source, target):
        one = pltpu.make_async_copy(source, target, sems.at[len(copies)])
        one.start()
        copies.append(one)

    for part in range(4):
        at = pl.ds(part * rows, rows)
        put(one_ref.at[at], one_hbm.at[at])
    wide = group * block
    narrow = wide // 4
    across = block // 2
    pixel = lax.broadcasted_iota(jnp.int32, (wide, narrow), 0)
    out = lax.broadcasted_iota(jnp.int32, (wide, narrow), 1)
    inside = (lax.div(pixel, block) * (across // 2) + lax.div(lax.rem(pixel, across), 2)) == out
    pool = jnp.where(inside, 0.25, 0.0).astype(jnp.bfloat16)
    for step in range(count // group):
        coarse = all_ref[step * group:(step + 1) * group, 1].reshape(wide, hidden)
        two = dot_last(upper_ref[...], coarse) + dot_last(lower_ref[...], coarse)
        two = (two + shift_ref[:, :1]).astype(jnp.bfloat16)
        two_ref[:, step * wide:(step + 1) * wide] = two
        three_ref[:, step * narrow:(step + 1) * narrow] = dot(two, pool).astype(jnp.bfloat16)
    put(two_ref, two_hbm)
    put(three_ref, three_hbm)
    for one in copies:
        one.wait()


def per_device(src_hidden, tgt_hidden, proj_weight, proj_bias):
    rows, width, hidden = tgt_hidden.shape
    channels = proj_weight.shape[1]
    count = lax.axis_size("tgt")
    own = src_hidden.shape[0]
    scale = 1.0 / math.sqrt(channels)
    fine_count = rows * width // 4
    lines = count // 4
    bias = proj_bias.reshape(1, channels)
    vmem = pl.BlockSpec(memory_space=pltpu.VMEM)
    hbm = pl.BlockSpec(memory_space=pltpu.HBM)
    gathered, one, upper, lower, shift = pl.pallas_call(
        functools.partial(gather_kernel, count, scale),
        out_shape=(
            jax.ShapeDtypeStruct((count, 2, own, hidden), jnp.bfloat16),
            jax.ShapeDtypeStruct((fine_count, own * count), jnp.bfloat16),
            jax.ShapeDtypeStruct((own, hidden), jnp.bfloat16),
            jax.ShapeDtypeStruct((own, hidden), jnp.bfloat16),
            jax.ShapeDtypeStruct((own, 128), jnp.float32),
        ),
        in_specs=[hbm] * 4,
        out_specs=(vmem,) * 5,
        scratch_shapes=[
            pltpu.VMEM(tgt_hidden.shape, jnp.bfloat16),
            pltpu.VMEM(proj_weight.shape, jnp.bfloat16),
            pltpu.VMEM(bias.shape, jnp.float32),
            pltpu.VMEM((fine_count, channels), jnp.bfloat16),
            pltpu.SemaphoreType.DMA((4,)),
            pltpu.SemaphoreType.DMA((2, 4 + 6 * (lines - 1) + 2 * lines)),
            pltpu.SemaphoreType.DMA((2, count)),
        ],
        compiler_params=pltpu.CompilerParams(
            collective_id=0, has_side_effects=True, vmem_limit_bytes=32 * 1024 * 1024
        ),
        name="gather",
    )(src_hidden, tgt_hidden, proj_weight, bias)
    two_count = fine_count // 4 * count
    one, two, three = pl.pallas_call(
        functools.partial(level_kernel, 4),
        out_shape=(
            jax.ShapeDtypeStruct((fine_count, own * count), jnp.bfloat16),
            jax.ShapeDtypeStruct((own, two_count), jnp.bfloat16),
            jax.ShapeDtypeStruct((own, two_count // 4), jnp.bfloat16),
        ),
        in_specs=[vmem] * 5,
        out_specs=(hbm,) * 3,
        scratch_shapes=[
            pltpu.VMEM((own, two_count), jnp.bfloat16),
            pltpu.VMEM((own, two_count // 4), jnp.bfloat16),
            pltpu.SemaphoreType.DMA((6,)),
        ],
        compiler_params=pltpu.CompilerParams(vmem_limit_bytes=32 * 1024 * 1024),
        name="levels",
    )(gathered, one, upper, lower, shift)
    return one.reshape(rows // 2, width // 2, own * count), two, three


def solution(mesh):
    return jax.shard_map(
        per_device,
        mesh=mesh,
        in_specs=(P(("pairs", "tgt"), None), P(("pairs", "tgt"), None, None), P(), P()),
        out_specs=(
            P(("pairs", "tgt"), None, None),
            P(("pairs", "tgt"), None),
            P(("pairs", "tgt"), None),
        ),
        check_vma=False,
    )
```

```python
import functools
import math

import jax
import jax.numpy as jnp
from jax import lax
from jax.experimental import pallas as pl
from jax.experimental.pallas import tpu as pltpu
from jax.sharding import PartitionSpec as P

MESH = pl.DeviceIdType.MESH
LAST = (((1,), (1,)), ((), ()))


def dot(left, right):
    return jnp.dot(left, right, preferred_element_type=jnp.float32)


def dot_last(left, right):
    return lax.dot_general(left, right, LAST, preferred_element_type=jnp.float32)


def split_parts(values):
    upper = values.astype(jnp.bfloat16)
    lower = (values - upper.astype(jnp.float32)).astype(jnp.bfloat16)
    return upper, lower


def pool_matrix(window, width):
    shape = (width // window, window * width)
    out = lax.broadcasted_iota(jnp.int32, shape, 0)
    pixel = lax.broadcasted_iota(jnp.int32, shape, 1)
    inside = lax.div(lax.rem(pixel, width), window) == out
    return jnp.where(inside, 1.0 / (window * window), 0.0).astype(jnp.bfloat16)


def gather_kernel(count, scale, src_hbm, tgt_hbm, weight_hbm, bias_hbm,
                  all_ref, fine_ref, upper_ref, lower_ref, shift_ref, weight_ref, bias_ref,
                  tgt_ref, load_sem, send_sem, recv_sem):
    rows, width, hidden = tgt_ref.shape
    lines = count // 4
    me = lax.axis_index("tgt")
    core = lax.rem(me, 2)
    mate = me + 1 - 2 * core
    side = lax.rem(lax.div(me, 2), 2)
    beside = me + 2 - 4 * side
    line = lax.div(me, 4)
    place = me - 4 * line

    def along(step):
        return 4 * lax.rem(line + step, lines) + place

    barrier = pltpu.get_barrier_semaphore()
    peers = [along(step) for step in range(1, lines)] + [beside, mate]
    for peer in peers:
        pl.semaphore_signal(barrier, inc=1, device_id={"tgt": peer}, device_id_type=MESH)
    loads = [
        pltpu.make_async_copy(tgt_hbm, tgt_ref, load_sem.at[0]),
        pltpu.make_async_copy(weight_hbm, weight_ref, load_sem.at[1]),
        pltpu.make_async_copy(bias_hbm, bias_ref, load_sem.at[2]),
        pltpu.make_async_copy(src_hbm, all_ref.at[me, 0], load_sem.at[3]),
    ]
    for load in loads:
        load.start()
    pl.semaphore_wait(barrier, len(peers))

    sent = []
    slots = [0, 0]

    def copy(part, block, peer, slot, first=False):
        return pltpu.make_async_remote_copy(
            src_ref=src_hbm if first else all_ref.at[block, part],
            dst_ref=all_ref.at[block, part],
            send_sem=send_sem.at[part, slot],
            recv_sem=recv_sem.at[part, block],
            device_id={"tgt": peer},
            device_id_type=MESH,
        )

    def send(part, block, peer, first=False):
        one = copy(part, block, peer, slots[part], first)
        slots[part] += 1
        one.start()
        sent.append(one)

    def arrive(part, block):
        copy(part, block, mate, 0).wait_recv()

    def own(part):
        first = part == 0
        send(part, me, beside, first)
        for step in range(1, lines):
            send(part, me, along(step), first)
        send(part, me, mate, first)

    own(0)
    coarse = pool_matrix(4, width)
    loads[0].wait()
    pooled = []
    for row in range(0, rows, 4):
        pooled.append(dot(coarse, tgt_ref[row:row + 4].reshape(4 * width, hidden)))
    all_ref[me, 1] = jnp.concatenate(pooled, axis=0).astype(jnp.bfloat16)
    own(1)
    for load in loads[1:]:
        load.wait()
    for part in (0, 1):
        for step in range(1, lines):
            block = along(lines - step)
            arrive(part, block)
            send(part, block, beside)
            send(part, block, mate)
        if part == 0:
            fine = pool_matrix(2, width)
            half = width // 2
            for row in range(0, rows, 2):
                upper, lower = split_parts(dot(fine, tgt_ref[row:row + 2].reshape(2 * width, hidden)))
                feat = dot(upper, weight_ref[...]) + dot(lower, weight_ref[...]) + bias_ref[...]
                fine_ref[row // 2 * half:(row // 2 + 1) * half] = (feat * scale).astype(jnp.bfloat16)
    for part in (0, 1):
        for step in range(lines):
            block = along((lines - step) % lines) + 2 - 4 * side
            arrive(part, block)
            send(part, block, mate)
    feat = (dot(all_ref[me, 0], weight_ref[...]) + bias_ref[...]).astype(jnp.bfloat16)
    upper, lower = split_parts(dot_last(feat, weight_ref[...]) * scale)
    upper_ref[...] = upper
    lower_ref[...] = lower
    shift = jnp.sum(feat.astype(jnp.float32) * bias_ref[...], axis=1, keepdims=True) * scale
    shift_ref[...] = jnp.broadcast_to(shift, shift_ref.shape)
    for part in (0, 1):
        for step in range(lines):
            block = along((lines - step) % lines) + 1 - 2 * core
            arrive(part, block)
            arrive(part, block + 2 - 4 * side)
    for one in sent:
        one.wait_send()


def level_kernel(group, all_ref, fine_ref, upper_ref, lower_ref, shift_ref, weight_ref, bias_ref,
                 one_hbm, two_hbm, three_hbm, one_ref, two_ref, three_ref, sems):
    count, _, block, hidden = all_ref.shape
    copies = []
    wide = group * block
    narrow = wide // 4
    across = block // 2
    pixel = lax.broadcasted_iota(jnp.int32, (wide, narrow), 0)
    out = lax.broadcasted_iota(jnp.int32, (wide, narrow), 1)
    inside = (lax.div(pixel, block) * (across // 2) + lax.div(lax.rem(pixel, across), 2)) == out
    pool = jnp.where(inside, 0.25, 0.0).astype(jnp.bfloat16)

    def put(source, target):
        one = pltpu.make_async_copy(source, target, sems.at[len(copies)])
        one.start()
        copies.append(one)

    for step in range(count // group):
        stripes = slice(step * group, (step + 1) * group)
        at = slice(step * wide, (step + 1) * wide)
        src = all_ref[stripes, 0].reshape(wide, hidden)
        feat = (dot(src, weight_ref[...]) + bias_ref[...]).astype(jnp.bfloat16)
        one_ref[:, at] = dot_last(fine_ref[...], feat).astype(jnp.bfloat16)
        put(one_ref.at[:, at], one_hbm.at[:, at])
    for step in range(count // group):
        stripes = slice(step * group, (step + 1) * group)
        at = slice(step * wide, (step + 1) * wide)
        coarse = all_ref[stripes, 1].reshape(wide, hidden)
        two = dot_last(upper_ref[...], coarse) + dot_last(lower_ref[...], coarse)
        two = (two + shift_ref[:, :1]).astype(jnp.bfloat16)
        two_ref[:, at] = two
        three_ref[:, step * narrow:(step + 1) * narrow] = dot(two, pool).astype(jnp.bfloat16)
    put(two_ref, two_hbm)
    put(three_ref, three_hbm)
    for one in copies:
        one.wait()


def per_device(src_hidden, tgt_hidden, proj_weight, proj_bias):
    rows, width, hidden = tgt_hidden.shape
    channels = proj_weight.shape[1]
    count = lax.axis_size("tgt")
    own = src_hidden.shape[0]
    scale = 1.0 / math.sqrt(channels)
    fine_count = rows * width // 4
    group = 4
    bias = proj_bias.reshape(1, channels)
    vmem = pl.BlockSpec(memory_space=pltpu.VMEM)
    hbm = pl.BlockSpec(memory_space=pltpu.HBM)
    between = (
        jax.ShapeDtypeStruct((count, 2, own, hidden), jnp.bfloat16),
        jax.ShapeDtypeStruct((fine_count, channels), jnp.bfloat16),
        jax.ShapeDtypeStruct((own, hidden), jnp.bfloat16),
        jax.ShapeDtypeStruct((own, hidden), jnp.bfloat16),
        jax.ShapeDtypeStruct((own, 128), jnp.float32),
        jax.ShapeDtypeStruct(proj_weight.shape, jnp.bfloat16),
        jax.ShapeDtypeStruct(bias.shape, jnp.float32),
    )
    arguments = [
        pltpu.with_memory_space_constraint(one, pltpu.HBM)
        for one in (src_hidden, tgt_hidden, proj_weight, bias)
    ]
    gathered = pl.pallas_call(
        functools.partial(gather_kernel, count, scale),
        out_shape=between,
        in_specs=[hbm] * 4,
        out_specs=(vmem,) * len(between),
        scratch_shapes=[
            pltpu.VMEM(tgt_hidden.shape, jnp.bfloat16),
            pltpu.SemaphoreType.DMA((4,)),
            pltpu.SemaphoreType.DMA((2, count)),
            pltpu.SemaphoreType.DMA((2, count)),
        ],
        compiler_params=pltpu.CompilerParams(
            collective_id=0, has_side_effects=True, vmem_limit_bytes=32 * 1024 * 1024
        ),
        name="gather",
    )(*arguments)
    two_count = fine_count // 4 * count
    levels = (
        jax.ShapeDtypeStruct((fine_count, own * count), jnp.bfloat16),
        jax.ShapeDtypeStruct((own, two_count), jnp.bfloat16),
        jax.ShapeDtypeStruct((own, two_count // 4), jnp.bfloat16),
    )
    one, two, three = pl.pallas_call(
        functools.partial(level_kernel, group),
        out_shape=levels,
        in_specs=[vmem] * len(between),
        out_specs=(hbm,) * 3,
        scratch_shapes=[pltpu.VMEM(level.shape, level.dtype) for level in levels]
        + [pltpu.SemaphoreType.DMA((count // group + 2,))],
        compiler_params=pltpu.CompilerParams(vmem_limit_bytes=32 * 1024 * 1024),
        name="levels",
    )(*gathered)
    return one.reshape(rows // 2, width // 2, own * count), two, three


def solution(mesh):
    return jax.shard_map(
        per_device,
        mesh=mesh,
        in_specs=(P(("pairs", "tgt"), None), P(("pairs", "tgt"), None, None), P(), P()),
        out_specs=(
            P(("pairs", "tgt"), None, None),
            P(("pairs", "tgt"), None),
            P(("pairs", "tgt"), None),
        ),
        check_vma=False,
    )
```

```python
import functools
import math

import jax
import jax.numpy as jnp
from jax import lax
from jax.experimental import pallas as pl
from jax.experimental.pallas import tpu as pltpu
from jax.sharding import PartitionSpec as P

MESH = pl.DeviceIdType.MESH
LAST = (((1,), (1,)), ((), ()))


def dot(left, right):
    return jnp.dot(left, right, preferred_element_type=jnp.float32)


def dot_last(left, right):
    return lax.dot_general(left, right, LAST, preferred_element_type=jnp.float32)


def split_parts(values):
    upper = values.astype(jnp.bfloat16)
    lower = (values - upper.astype(jnp.float32)).astype(jnp.bfloat16)
    return upper, lower


def pool_matrix(window, width):
    shape = (width // window, window * width)
    out = lax.broadcasted_iota(jnp.int32, shape, 0)
    pixel = lax.broadcasted_iota(jnp.int32, shape, 1)
    inside = lax.div(lax.rem(pixel, width), window) == out
    return jnp.where(inside, 1.0 / (window * window), 0.0).astype(jnp.bfloat16)


def gather_kernel(count, scale, src_hbm, tgt_hbm, weight_hbm, bias_hbm,
                  all_ref, fine_ref, upper_ref, lower_ref, shift_ref, weight_ref, bias_ref,
                  tgt_ref, load_sem, send_sem, recv_sem):
    rows, width, hidden = tgt_ref.shape
    lines = count // 8
    me = lax.axis_index("tgt")
    to_mate = 1 - 2 * lax.rem(me, 2)
    to_beside = 2 - 4 * lax.rem(lax.div(me, 2), 2)
    to_near = 4 - 8 * lax.rem(lax.div(me, 4), 2)
    mate, beside, near = me + to_mate, me + to_beside, me + to_near
    line = lax.div(me, 8)
    place = me - 8 * line

    def along(step):
        return 8 * lax.rem(line + step, lines) + place

    barrier = pltpu.get_barrier_semaphore()
    peers = [along(step) for step in range(1, lines)] + [near, beside, mate]
    for peer in peers:
        pl.semaphore_signal(barrier, inc=1, device_id={"tgt": peer}, device_id_type=MESH)
    loads = [
        pltpu.make_async_copy(tgt_hbm, tgt_ref, load_sem.at[0]),
        pltpu.make_async_copy(weight_hbm, weight_ref, load_sem.at[1]),
        pltpu.make_async_copy(bias_hbm, bias_ref, load_sem.at[2]),
        pltpu.make_async_copy(src_hbm, all_ref.at[me, 0], load_sem.at[3]),
    ]
    for load in loads:
        load.start()
    pl.semaphore_wait(barrier, len(peers))

    sent = []
    slots = [0, 0]

    def copy(part, block, peer, slot, first=False):
        return pltpu.make_async_remote_copy(
            src_ref=src_hbm if first else all_ref.at[block, part],
            dst_ref=all_ref.at[block, part],
            send_sem=send_sem.at[part, slot],
            recv_sem=recv_sem.at[part, block],
            device_id={"tgt": peer},
            device_id_type=MESH,
        )

    def send(part, block, peer, first=False):
        one = copy(part, block, peer, slots[part], first)
        slots[part] += 1
        one.start()
        sent.append(one)

    def arrive(part, block):
        copy(part, block, mate, 0).wait_recv()

    def own(part):
        first = part == 0
        send(part, me, beside, first)
        for step in range(1, lines):
            send(part, me, along(step), first)
        send(part, me, near, first)
        send(part, me, mate, first)

    own(0)
    coarse = pool_matrix(4, width)
    loads[0].wait()
    pooled = []
    for row in range(0, rows, 4):
        pooled.append(dot(coarse, tgt_ref[row:row + 4].reshape(4 * width, hidden)))
    all_ref[me, 1] = jnp.concatenate(pooled, axis=0).astype(jnp.bfloat16)
    own(1)
    for load in loads[1:]:
        load.wait()
    fine = pool_matrix(2, width)
    half = width // 2
    for part in (0, 1):
        block = me + to_near
        arrive(part, block)
        send(part, block, beside)
        send(part, block, mate)
        for step in range(1, lines):
            block = along(lines - step)
            arrive(part, block)
            send(part, block, near)
            send(part, block, beside)
            send(part, block, mate)
        if part == 0:
            for row in range(0, rows, 2):
                upper, lower = split_parts(dot(fine, tgt_ref[row:row + 2].reshape(2 * width, hidden)))
                feat = dot(upper, weight_ref[...]) + dot(lower, weight_ref[...]) + bias_ref[...]
                fine_ref[row // 2 * half:(row // 2 + 1) * half] = (feat * scale).astype(jnp.bfloat16)
    for part in (0, 1):
        for step in range(1, lines):
            block = along(lines - step) + to_near
            arrive(part, block)
            send(part, block, beside)
            send(part, block, mate)
    for part in (0, 1):
        for step in range(lines):
            block = along((lines - step) % lines) + to_beside
            for block in (block, block + to_near):
                arrive(part, block)
                send(part, block, mate)
    feat = (dot(all_ref[me, 0], weight_ref[...]) + bias_ref[...]).astype(jnp.bfloat16)
    upper, lower = split_parts(dot_last(feat, weight_ref[...]) * scale)
    upper_ref[...] = upper
    lower_ref[...] = lower
    shift = jnp.sum(feat.astype(jnp.float32) * bias_ref[...], axis=1, keepdims=True) * scale
    shift_ref[...] = jnp.broadcast_to(shift, shift_ref.shape)
    for part in (0, 1):
        for step in range(lines):
            block = along((lines - step) % lines) + to_mate
            for block in (block, block + to_near):
                arrive(part, block)
                arrive(part, block + to_beside)
    for one in sent:
        one.wait_send()


def level_kernel(group, all_ref, fine_ref, upper_ref, lower_ref, shift_ref, weight_ref, bias_ref,
                 one_hbm, two_hbm, three_hbm, one_ref, two_ref, three_ref, sems):
    count, _, block, hidden = all_ref.shape
    copies = []
    wide = group * block
    narrow = wide // 4
    across = block // 2
    pixel = lax.broadcasted_iota(jnp.int32, (wide, narrow), 0)
    out = lax.broadcasted_iota(jnp.int32, (wide, narrow), 1)
    inside = (lax.div(pixel, block) * (across // 2) + lax.div(lax.rem(pixel, across), 2)) == out
    pool = jnp.where(inside, 0.25, 0.0).astype(jnp.bfloat16)

    def put(source, target):
        one = pltpu.make_async_copy(source, target, sems.at[len(copies)])
        one.start()
        copies.append(one)

    for step in range(count // group):
        stripes = slice(step * group, (step + 1) * group)
        at = slice(step * wide, (step + 1) * wide)
        src = all_ref[stripes, 0].reshape(wide, hidden)
        feat = (dot(src, weight_ref[...]) + bias_ref[...]).astype(jnp.bfloat16)
        one_ref[:, at] = dot_last(fine_ref[...], feat).astype(jnp.bfloat16)
        put(one_ref.at[:, at], one_hbm.at[:, at])
    for step in range(count // group):
        stripes = slice(step * group, (step + 1) * group)
        at = slice(step * wide, (step + 1) * wide)
        coarse = all_ref[stripes, 1].reshape(wide, hidden)
        two = dot_last(upper_ref[...], coarse) + dot_last(lower_ref[...], coarse)
        two = (two + shift_ref[:, :1]).astype(jnp.bfloat16)
        two_ref[:, at] = two
        three_ref[:, step * narrow:(step + 1) * narrow] = dot(two, pool).astype(jnp.bfloat16)
    put(two_ref, two_hbm)
    put(three_ref, three_hbm)
    for one in copies:
        one.wait()


def per_device(src_hidden, tgt_hidden, proj_weight, proj_bias):
    rows, width, hidden = tgt_hidden.shape
    channels = proj_weight.shape[1]
    count = lax.axis_size("tgt")
    own = src_hidden.shape[0]
    scale = 1.0 / math.sqrt(channels)
    fine_count = rows * width // 4
    group = 4
    bias = proj_bias.reshape(1, channels)
    vmem = pl.BlockSpec(memory_space=pltpu.VMEM)
    hbm = pl.BlockSpec(memory_space=pltpu.HBM)
    between = (
        jax.ShapeDtypeStruct((count, 2, own, hidden), jnp.bfloat16),
        jax.ShapeDtypeStruct((fine_count, channels), jnp.bfloat16),
        jax.ShapeDtypeStruct((own, hidden), jnp.bfloat16),
        jax.ShapeDtypeStruct((own, hidden), jnp.bfloat16),
        jax.ShapeDtypeStruct((own, 128), jnp.float32),
        jax.ShapeDtypeStruct(proj_weight.shape, jnp.bfloat16),
        jax.ShapeDtypeStruct(bias.shape, jnp.float32),
    )
    arguments = [
        pltpu.with_memory_space_constraint(one, pltpu.HBM)
        for one in (src_hidden, tgt_hidden, proj_weight, bias)
    ]
    gathered = pl.pallas_call(
        functools.partial(gather_kernel, count, scale),
        out_shape=between,
        in_specs=[hbm] * 4,
        out_specs=(vmem,) * len(between),
        scratch_shapes=[
            pltpu.VMEM(tgt_hidden.shape, jnp.bfloat16),
            pltpu.SemaphoreType.DMA((4,)),
            pltpu.SemaphoreType.DMA((2, count)),
            pltpu.SemaphoreType.DMA((2, count)),
        ],
        compiler_params=pltpu.CompilerParams(
            collective_id=0, has_side_effects=True, vmem_limit_bytes=32 * 1024 * 1024
        ),
        name="gather",
    )(*arguments)
    two_count = fine_count // 4 * count
    levels = (
        jax.ShapeDtypeStruct((fine_count, own * count), jnp.bfloat16),
        jax.ShapeDtypeStruct((own, two_count), jnp.bfloat16),
        jax.ShapeDtypeStruct((own, two_count // 4), jnp.bfloat16),
    )
    one, two, three = pl.pallas_call(
        functools.partial(level_kernel, group),
        out_shape=levels,
        in_specs=[vmem] * len(between),
        out_specs=(hbm,) * 3,
        scratch_shapes=[pltpu.VMEM(level.shape, level.dtype) for level in levels]
        + [pltpu.SemaphoreType.DMA((count // group + 2,))],
        compiler_params=pltpu.CompilerParams(vmem_limit_bytes=32 * 1024 * 1024),
        name="levels",
    )(*gathered)
    return one.reshape(rows // 2, width // 2, own * count), two, three


def solution(mesh):
    return jax.shard_map(
        per_device,
        mesh=mesh,
        in_specs=(P(("pairs", "tgt"), None), P(("pairs", "tgt"), None, None), P(), P()),
        out_specs=(
            P(("pairs", "tgt"), None, None),
            P(("pairs", "tgt"), None),
            P(("pairs", "tgt"), None),
        ),
        check_vma=False,
    )
```

```python
import functools
import math

import jax
import jax.numpy as jnp
from jax import lax
from jax.experimental import pallas as pl
from jax.experimental.pallas import tpu as pltpu
from jax.sharding import PartitionSpec as P

MESH = pl.DeviceIdType.MESH
LAST = (((1,), (1,)), ((), ()))


def dot(left, right):
    return jnp.dot(left, right, preferred_element_type=jnp.float32)


def dot_last(left, right):
    return lax.dot_general(left, right, LAST, preferred_element_type=jnp.float32)


def split_parts(values):
    upper = values.astype(jnp.bfloat16)
    lower = (values - upper.astype(jnp.float32)).astype(jnp.bfloat16)
    return upper, lower


def pool_matrix(window, width):
    shape = (width // window, window * width)
    out = lax.broadcasted_iota(jnp.int32, shape, 0)
    pixel = lax.broadcasted_iota(jnp.int32, shape, 1)
    inside = lax.div(lax.rem(pixel, width), window) == out
    return jnp.where(inside, 1.0 / (window * window), 0.0).astype(jnp.bfloat16)


def gather_kernel(count, scale, src_hbm, tgt_hbm, weight_hbm, bias_hbm,
                  all_ref, fine_ref, upper_ref, lower_ref, shift_ref, weight_ref, bias_ref,
                  one_ref, tgt_ref, load_sem, send_sem, recv_sem):
    rows, width, hidden = tgt_ref.shape
    lines = count // 8
    me = lax.axis_index("tgt")
    to_mate = 1 - 2 * lax.rem(me, 2)
    to_beside = 2 - 4 * lax.rem(lax.div(me, 2), 2)
    to_near = 4 - 8 * lax.rem(lax.div(me, 4), 2)
    mate, beside, near = me + to_mate, me + to_beside, me + to_near
    line = lax.div(me, 8)
    place = me - 8 * line

    def along(step):
        return 8 * lax.rem(line + step, lines) + place

    barrier = pltpu.get_barrier_semaphore()
    peers = [along(step) for step in range(1, lines)] + [near, beside, mate]
    for peer in peers:
        pl.semaphore_signal(barrier, inc=1, device_id={"tgt": peer}, device_id_type=MESH)
    loads = [
        pltpu.make_async_copy(tgt_hbm, tgt_ref, load_sem.at[0]),
        pltpu.make_async_copy(weight_hbm, weight_ref, load_sem.at[1]),
        pltpu.make_async_copy(bias_hbm, bias_ref, load_sem.at[2]),
        pltpu.make_async_copy(src_hbm, all_ref.at[me, 0], load_sem.at[3]),
    ]
    for load in loads:
        load.start()
    pl.semaphore_wait(barrier, len(peers))

    sent = []
    slots = [0, 0]

    def copy(part, block, peer, slot, first=False):
        return pltpu.make_async_remote_copy(
            src_ref=src_hbm if first else all_ref.at[block, part],
            dst_ref=all_ref.at[block, part],
            send_sem=send_sem.at[part, slot],
            recv_sem=recv_sem.at[part, block],
            device_id={"tgt": peer},
            device_id_type=MESH,
        )

    def send(part, block, peer, first=False):
        one = copy(part, block, peer, slots[part], first)
        slots[part] += 1
        one.start()
        sent.append(one)

    def arrive(part, block):
        copy(part, block, mate, 0).wait_recv()

    def own(part):
        first = part == 0
        send(part, me, beside, first)
        for step in range(1, lines):
            send(part, me, along(step), first)
        send(part, me, near, first)
        send(part, me, mate, first)

    def level_one(block):
        width = src_hbm.shape[0]
        feat = (dot(all_ref[block, 0], weight_ref[...]) + bias_ref[...]).astype(jnp.bfloat16)
        at = pl.ds(pl.multiple_of(block * width, width), width)
        one_ref[:, at] = dot_last(fine_ref[...], feat).astype(jnp.bfloat16)

    own(0)
    coarse = pool_matrix(4, width)
    loads[0].wait()
    pooled = []
    for row in range(0, rows, 4):
        pooled.append(dot(coarse, tgt_ref[row:row + 4].reshape(4 * width, hidden)))
    all_ref[me, 1] = jnp.concatenate(pooled, axis=0).astype(jnp.bfloat16)
    own(1)
    for load in loads[1:]:
        load.wait()
    fine = pool_matrix(2, width)
    half = width // 2
    for part in (0, 1):
        block = me + to_near
        arrive(part, block)
        send(part, block, beside)
        send(part, block, mate)
        for step in range(1, lines):
            block = along(lines - step)
            arrive(part, block)
            send(part, block, near)
            send(part, block, beside)
            send(part, block, mate)
        if part == 0:
            for row in range(0, rows, 2):
                upper, lower = split_parts(dot(fine, tgt_ref[row:row + 2].reshape(2 * width, hidden)))
                feat = dot(upper, weight_ref[...]) + dot(lower, weight_ref[...]) + bias_ref[...]
                fine_ref[row // 2 * half:(row // 2 + 1) * half] = (feat * scale).astype(jnp.bfloat16)
    level_one(me)
    level_one(near)
    for part in (0, 1):
        for step in range(1, lines):
            block = along(lines - step) + to_near
            arrive(part, block)
            send(part, block, beside)
            send(part, block, mate)
    for step in range(1, lines):
        level_one(along(step))
        level_one(along(step) + to_near)
    for part in (0, 1):
        for step in range(lines):
            block = along((lines - step) % lines) + to_beside
            for block in (block, block + to_near):
                arrive(part, block)
                send(part, block, mate)
    feat = (dot(all_ref[me, 0], weight_ref[...]) + bias_ref[...]).astype(jnp.bfloat16)
    upper, lower = split_parts(dot_last(feat, weight_ref[...]) * scale)
    upper_ref[...] = upper
    lower_ref[...] = lower
    shift = jnp.sum(feat.astype(jnp.float32) * bias_ref[...], axis=1, keepdims=True) * scale
    shift_ref[...] = jnp.broadcast_to(shift, shift_ref.shape)
    for step in range(lines):
        block = along((lines - step) % lines)
        for block in (block, block + to_near):
            level_one(block + to_beside)
            arrive(0, block + to_mate)
            level_one(block + to_mate)
    for step in range(lines):
        block = along((lines - step) % lines) + to_mate
        for block in (block, block + to_near):
            arrive(1, block)
            arrive(0, block + to_beside)
            arrive(1, block + to_beside)
    for one in sent:
        one.wait_send()


def level_kernel(group, all_ref, fine_ref, upper_ref, lower_ref, shift_ref, weight_ref, bias_ref,
                 early_ref, one_hbm, two_hbm, three_hbm, one_ref, two_ref, three_ref, sems):
    count, _, block, hidden = all_ref.shape
    copies = []
    wide = group * block
    narrow = wide // 4
    across = block // 2

    def put(source, target):
        one = pltpu.make_async_copy(source, target, sems.at[len(copies)])
        one.start()
        copies.append(one)

    late = 3 - lax.rem(lax.axis_index("tgt"), 4)

    def columns(index):
        return pl.ds(pl.multiple_of(index * block, block), block)

    for line in range(count // 4):
        for other in range(1, 4):
            at = columns(4 * line + lax.rem(late + other, 4))
            put(early_ref.at[:, at], one_hbm.at[:, at])
    for line in range(0, count // 4, 2):
        src = [all_ref[4 * each + late, 0] for each in (line, line + 1)]
        feat = (dot(jnp.concatenate(src, axis=0), weight_ref[...]) + bias_ref[...]).astype(jnp.bfloat16)
        one_ref[:, line * block:(line + 2) * block] = dot_last(fine_ref[...], feat).astype(jnp.bfloat16)
        for each in (line, line + 1):
            put(one_ref.at[:, pl.ds(each * block, block)], one_hbm.at[:, columns(4 * each + late)])
    pixel = lax.broadcasted_iota(jnp.int32, (wide, narrow), 0)
    out = lax.broadcasted_iota(jnp.int32, (wide, narrow), 1)
    inside = (lax.div(pixel, block) * (across // 2) + lax.div(lax.rem(pixel, across), 2)) == out
    pool = jnp.where(inside, 0.25, 0.0).astype(jnp.bfloat16)
    for step in range(count // group):
        stripes = slice(step * group, (step + 1) * group)
        at = slice(step * wide, (step + 1) * wide)
        coarse = all_ref[stripes, 1].reshape(wide, hidden)
        two = dot_last(upper_ref[...], coarse) + dot_last(lower_ref[...], coarse)
        two = (two + shift_ref[:, :1]).astype(jnp.bfloat16)
        two_ref[:, at] = two
        three_ref[:, step * narrow:(step + 1) * narrow] = dot(two, pool).astype(jnp.bfloat16)
    put(two_ref, two_hbm)
    put(three_ref, three_hbm)
    for one in copies:
        one.wait()


def per_device(src_hidden, tgt_hidden, proj_weight, proj_bias):
    rows, width, hidden = tgt_hidden.shape
    channels = proj_weight.shape[1]
    count = lax.axis_size("tgt")
    own = src_hidden.shape[0]
    scale = 1.0 / math.sqrt(channels)
    fine_count = rows * width // 4
    group = 4
    bias = proj_bias.reshape(1, channels)
    vmem = pl.BlockSpec(memory_space=pltpu.VMEM)
    hbm = pl.BlockSpec(memory_space=pltpu.HBM)
    between = (
        jax.ShapeDtypeStruct((count, 2, own, hidden), jnp.bfloat16),
        jax.ShapeDtypeStruct((fine_count, channels), jnp.bfloat16),
        jax.ShapeDtypeStruct((own, hidden), jnp.bfloat16),
        jax.ShapeDtypeStruct((own, hidden), jnp.bfloat16),
        jax.ShapeDtypeStruct((own, 128), jnp.float32),
        jax.ShapeDtypeStruct(proj_weight.shape, jnp.bfloat16),
        jax.ShapeDtypeStruct(bias.shape, jnp.float32),
        jax.ShapeDtypeStruct((fine_count, own * count), jnp.bfloat16),
    )
    arguments = [
        pltpu.with_memory_space_constraint(one, pltpu.HBM)
        for one in (src_hidden, tgt_hidden, proj_weight, bias)
    ]
    gathered = pl.pallas_call(
        functools.partial(gather_kernel, count, scale),
        out_shape=between,
        in_specs=[hbm] * 4,
        out_specs=(vmem,) * len(between),
        scratch_shapes=[
            pltpu.VMEM(tgt_hidden.shape, jnp.bfloat16),
            pltpu.SemaphoreType.DMA((4,)),
            pltpu.SemaphoreType.DMA((2, count)),
            pltpu.SemaphoreType.DMA((2, count)),
        ],
        compiler_params=pltpu.CompilerParams(
            collective_id=0, has_side_effects=True, vmem_limit_bytes=32 * 1024 * 1024
        ),
        name="gather",
    )(*arguments)
    two_count = fine_count // 4 * count
    levels = (
        jax.ShapeDtypeStruct((fine_count, own * count), jnp.bfloat16),
        jax.ShapeDtypeStruct((own, two_count), jnp.bfloat16),
        jax.ShapeDtypeStruct((own, two_count // 4), jnp.bfloat16),
    )
    one, two, three = pl.pallas_call(
        functools.partial(level_kernel, group),
        out_shape=levels,
        in_specs=[vmem] * len(between),
        out_specs=(hbm,) * 3,
        scratch_shapes=[
            pltpu.VMEM((fine_count, own * count // 4), jnp.bfloat16),
            pltpu.VMEM((own, two_count), jnp.bfloat16),
            pltpu.VMEM((own, two_count // 4), jnp.bfloat16),
            pltpu.SemaphoreType.DMA((count + 2,)),
        ],
        compiler_params=pltpu.CompilerParams(vmem_limit_bytes=32 * 1024 * 1024),
        name="levels",
    )(*gathered)
    return one.reshape(rows // 2, width // 2, own * count), two, three


def solution(mesh):
    return jax.shard_map(
        per_device,
        mesh=mesh,
        in_specs=(P(("pairs", "tgt"), None), P(("pairs", "tgt"), None, None), P(), P()),
        out_specs=(
            P(("pairs", "tgt"), None, None),
            P(("pairs", "tgt"), None),
            P(("pairs", "tgt"), None),
        ),
        check_vma=False,
    )
```

```python
import functools
import math

import jax
import jax.numpy as jnp
from jax import lax
from jax.experimental import pallas as pl
from jax.experimental.pallas import tpu as pltpu
from jax.sharding import PartitionSpec as P

MESH = pl.DeviceIdType.MESH
LAST = (((1,), (1,)), ((), ()))


def dot(left, right):
    return jnp.dot(left, right, preferred_element_type=jnp.float32)


def dot_last(left, right):
    return lax.dot_general(left, right, LAST, preferred_element_type=jnp.float32)


def split_parts(values):
    upper = values.astype(jnp.bfloat16)
    lower = (values - upper.astype(jnp.float32)).astype(jnp.bfloat16)
    return upper, lower


def pool_matrix(window, width):
    shape = (width // window, window * width)
    out = lax.broadcasted_iota(jnp.int32, shape, 0)
    pixel = lax.broadcasted_iota(jnp.int32, shape, 1)
    inside = lax.div(lax.rem(pixel, width), window) == out
    return jnp.where(inside, 1.0 / (window * window), 0.0).astype(jnp.bfloat16)


def gather_kernel(count, scale, src_hbm, tgt_hbm, weight_hbm, bias_hbm,
                  all_ref, fine_ref, upper_ref, lower_ref, shift_ref, weight_ref, bias_ref,
                  one_ref, tgt_ref, load_sem, send_sem, recv_sem):
    rows, width, hidden = tgt_ref.shape
    lines = count // 8
    me = lax.axis_index("tgt")
    to_mate = 1 - 2 * lax.rem(me, 2)
    to_beside = 2 - 4 * lax.rem(lax.div(me, 2), 2)
    to_near = 4 - 8 * lax.rem(lax.div(me, 4), 2)
    mate, beside, near = me + to_mate, me + to_beside, me + to_near
    line = lax.div(me, 8)
    place = me - 8 * line

    def along(step):
        return 8 * lax.rem(line + step, lines) + place

    barrier = pltpu.get_barrier_semaphore()
    peers = [along(step) for step in range(1, lines)] + [near, beside, mate]
    for peer in peers:
        pl.semaphore_signal(barrier, inc=1, device_id={"tgt": peer}, device_id_type=MESH)
    loads = [
        pltpu.make_async_copy(tgt_hbm, tgt_ref, load_sem.at[0]),
        pltpu.make_async_copy(weight_hbm, weight_ref, load_sem.at[1]),
        pltpu.make_async_copy(bias_hbm, bias_ref, load_sem.at[2]),
        pltpu.make_async_copy(src_hbm, all_ref.at[me, 0], load_sem.at[3]),
    ]
    for load in loads:
        load.start()
    pl.semaphore_wait(barrier, len(peers))

    sent = []
    slots = [0, 0]

    def copy(part, block, peer, slot, first=False):
        return pltpu.make_async_remote_copy(
            src_ref=src_hbm if first else all_ref.at[block, part],
            dst_ref=all_ref.at[block, part],
            send_sem=send_sem.at[part, slot],
            recv_sem=recv_sem.at[part, block],
            device_id={"tgt": peer},
            device_id_type=MESH,
        )

    def send(part, block, peer, first=False):
        one = copy(part, block, peer, slots[part], first)
        slots[part] += 1
        one.start()
        sent.append(one)

    def arrive(part, block):
        copy(part, block, mate, 0).wait_recv()

    def own(part):
        first = part == 0
        send(part, me, beside, first)
        for step in range(1, lines):
            send(part, me, along(step), first)
        send(part, me, near, first)
        send(part, me, mate, first)

    def level_one(block):
        width = src_hbm.shape[0]
        feat = (dot(all_ref[block, 0], weight_ref[...]) + bias_ref[...]).astype(jnp.bfloat16)
        at = pl.ds(pl.multiple_of(block * width, width), width)
        one_ref[:, at] = dot_last(fine_ref[...], feat).astype(jnp.bfloat16)

    own(0)
    coarse = pool_matrix(4, width)
    loads[0].wait()
    pooled = []
    for row in range(0, rows, 4):
        pooled.append(dot(coarse, tgt_ref[row:row + 4].reshape(4 * width, hidden)))
    all_ref[me, 1] = jnp.concatenate(pooled, axis=0).astype(jnp.bfloat16)
    own(1)
    for load in loads[1:]:
        load.wait()
    fine = pool_matrix(2, width)
    half = width // 2
    for part in (0, 1):
        block = me + to_near
        arrive(part, block)
        send(part, block, beside)
        send(part, block, mate)
        for step in range(1, lines):
            block = along(lines - step)
            arrive(part, block)
            send(part, block, near)
            send(part, block, beside)
            send(part, block, mate)
        if part == 0:
            for row in range(0, rows, 2):
                upper, lower = split_parts(dot(fine, tgt_ref[row:row + 2].reshape(2 * width, hidden)))
                feat = dot(upper, weight_ref[...]) + dot(lower, weight_ref[...]) + bias_ref[...]
                fine_ref[row // 2 * half:(row // 2 + 1) * half] = (feat * scale).astype(jnp.bfloat16)
    for part in (0, 1):
        for step in range(1, lines):
            block = along(lines - step) + to_near
            arrive(part, block)
            send(part, block, beside)
            send(part, block, mate)
    for part in (0, 1):
        for step in range(lines):
            block = along((lines - step) % lines) + to_beside
            for block in (block, block + to_near):
                arrive(part, block)
                send(part, block, mate)
    feat = (dot(all_ref[me, 0], weight_ref[...]) + bias_ref[...]).astype(jnp.bfloat16)
    upper, lower = split_parts(dot_last(feat, weight_ref[...]) * scale)
    upper_ref[...] = upper
    lower_ref[...] = lower
    shift = jnp.sum(feat.astype(jnp.float32) * bias_ref[...], axis=1, keepdims=True) * scale
    shift_ref[...] = jnp.broadcast_to(shift, shift_ref.shape)
    for step in range(lines):
        block = along((lines - step) % lines)
        for block in (block, block + to_near):
            level_one(block)
            level_one(block + to_beside)
    for part in (0, 1):
        for step in range(lines):
            block = along((lines - step) % lines) + to_mate
            for block in (block, block + to_near):
                arrive(part, block)
                arrive(part, block + to_beside)
    for one in sent:
        one.wait_send()


def level_kernel(group, all_ref, fine_ref, upper_ref, lower_ref, shift_ref, weight_ref, bias_ref,
                 early_ref, one_hbm, two_hbm, three_hbm, one_ref, two_ref, three_ref, sems):
    count, _, block, hidden = all_ref.shape
    copies = []
    wide = group * block
    narrow = wide // 4
    across = block // 2

    def put(source, target):
        one = pltpu.make_async_copy(source, target, sems.at[len(copies)])
        one.start()
        copies.append(one)

    core = lax.rem(lax.axis_index("tgt"), 2)

    def columns(index):
        return pl.ds(pl.multiple_of(index * block, block), block)

    for pair in range(count // 2):
        at = columns(2 * pair + core)
        put(early_ref.at[:, at], one_hbm.at[:, at])
    for first in range(0, count // 2, group):
        pairs = range(first, first + group)
        src = jnp.concatenate([all_ref[2 * pair + 1 - core, 0] for pair in pairs], axis=0)
        feat = (dot(src, weight_ref[...]) + bias_ref[...]).astype(jnp.bfloat16)
        one_ref[:, first * block:(first + group) * block] = dot_last(fine_ref[...], feat).astype(jnp.bfloat16)
        for pair in pairs:
            put(one_ref.at[:, pl.ds(pair * block, block)], one_hbm.at[:, columns(2 * pair + 1 - core)])
    pixel = lax.broadcasted_iota(jnp.int32, (wide, narrow), 0)
    out = lax.broadcasted_iota(jnp.int32, (wide, narrow), 1)
    inside = (lax.div(pixel, block) * (across // 2) + lax.div(lax.rem(pixel, across), 2)) == out
    pool = jnp.where(inside, 0.25, 0.0).astype(jnp.bfloat16)
    for step in range(count // group):
        stripes = slice(step * group, (step + 1) * group)
        at = slice(step * wide, (step + 1) * wide)
        coarse = all_ref[stripes, 1].reshape(wide, hidden)
        two = dot_last(upper_ref[...], coarse) + dot_last(lower_ref[...], coarse)
        two = (two + shift_ref[:, :1]).astype(jnp.bfloat16)
        two_ref[:, at] = two
        three_ref[:, step * narrow:(step + 1) * narrow] = dot(two, pool).astype(jnp.bfloat16)
    put(two_ref, two_hbm)
    put(three_ref, three_hbm)
    for one in copies:
        one.wait()


def per_device(src_hidden, tgt_hidden, proj_weight, proj_bias):
    rows, width, hidden = tgt_hidden.shape
    channels = proj_weight.shape[1]
    count = lax.axis_size("tgt")
    own = src_hidden.shape[0]
    scale = 1.0 / math.sqrt(channels)
    fine_count = rows * width // 4
    group = 4
    bias = proj_bias.reshape(1, channels)
    vmem = pl.BlockSpec(memory_space=pltpu.VMEM)
    hbm = pl.BlockSpec(memory_space=pltpu.HBM)
    between = (
        jax.ShapeDtypeStruct((count, 2, own, hidden), jnp.bfloat16),
        jax.ShapeDtypeStruct((fine_count, channels), jnp.bfloat16),
        jax.ShapeDtypeStruct((own, hidden), jnp.bfloat16),
        jax.ShapeDtypeStruct((own, hidden), jnp.bfloat16),
        jax.ShapeDtypeStruct((own, 128), jnp.float32),
        jax.ShapeDtypeStruct(proj_weight.shape, jnp.bfloat16),
        jax.ShapeDtypeStruct(bias.shape, jnp.float32),
        jax.ShapeDtypeStruct((fine_count, own * count), jnp.bfloat16),
    )
    arguments = [
        pltpu.with_memory_space_constraint(one, pltpu.HBM)
        for one in (src_hidden, tgt_hidden, proj_weight, bias)
    ]
    gathered = pl.pallas_call(
        functools.partial(gather_kernel, count, scale),
        out_shape=between,
        in_specs=[hbm] * 4,
        out_specs=(vmem,) * len(between),
        scratch_shapes=[
            pltpu.VMEM(tgt_hidden.shape, jnp.bfloat16),
            pltpu.SemaphoreType.DMA((4,)),
            pltpu.SemaphoreType.DMA((2, count)),
            pltpu.SemaphoreType.DMA((2, count)),
        ],
        compiler_params=pltpu.CompilerParams(
            collective_id=0, has_side_effects=True, vmem_limit_bytes=32 * 1024 * 1024
        ),
        name="gather",
    )(*arguments)
    two_count = fine_count // 4 * count
    levels = (
        jax.ShapeDtypeStruct((fine_count, own * count), jnp.bfloat16),
        jax.ShapeDtypeStruct((own, two_count), jnp.bfloat16),
        jax.ShapeDtypeStruct((own, two_count // 4), jnp.bfloat16),
    )
    one, two, three = pl.pallas_call(
        functools.partial(level_kernel, group),
        out_shape=levels,
        in_specs=[vmem] * len(between),
        out_specs=(hbm,) * 3,
        scratch_shapes=[
            pltpu.VMEM((fine_count, own * count // 2), jnp.bfloat16),
            pltpu.VMEM((own, two_count), jnp.bfloat16),
            pltpu.VMEM((own, two_count // 4), jnp.bfloat16),
            pltpu.SemaphoreType.DMA((count + 2,)),
        ],
        compiler_params=pltpu.CompilerParams(vmem_limit_bytes=32 * 1024 * 1024),
        name="levels",
    )(*gathered)
    return one.reshape(rows // 2, width // 2, own * count), two, three


def solution(mesh):
    return jax.shard_map(
        per_device,
        mesh=mesh,
        in_specs=(P(("pairs", "tgt"), None), P(("pairs", "tgt"), None, None), P(), P()),
        out_specs=(
            P(("pairs", "tgt"), None, None),
            P(("pairs", "tgt"), None),
            P(("pairs", "tgt"), None),
        ),
        check_vma=False,
    )
```
